32 devices in a mesh: wide: 8 (over z, y), narrow: 4 (over x, core).
Axes of the slice: x: 2, y: 2, z: 4, core: 2. Of those that a mesh axis runs over, the one named last changes fastest.
Arguments:
- inputs: bfloat16 [768, 12288], P('narrow', 'wide'), may hold values from -50 to 50
- clip_bounds: int32 [2, 12288], P(None, 'wide'), may hold values from 0 to 12288, as said below
- qkv_weight: bfloat16 [2, 3, 768, 768], P(None, None, 'wide', 'narrow'), may hold values from -0.21875 to 0.21875
- out_weight: bfloat16 [2, 768, 768], P(None, 'narrow', 'wide'), may hold values from -0.875 to 0.875
- fc1_weight: bfloat16 [2, 768, 3072], P(None, 'wide', 'narrow'), may hold values from -0.21875 to 0.21875
- fc2_weight: bfloat16 [2, 3072, 768], P(None, 'narrow', 'wide'), may hold values from -0.109375 to 0.109375
- gains: bfloat16 [2, 2, 768], P(None, None, ('narrow', 'wide')), may hold values from 0.25 to 1.75
- biases: bfloat16 [2, 6, 768], P(None, None, ('narrow', 'wide')), may hold values from -2 to 2
- fc1_bias: bfloat16 [2, 3072], P(None, ('narrow', 'wide')), may hold values from -2 to 2
- cotangent: bfloat16 [768, 12288], P('narrow', 'wide'), may hold values from -6 to 6
Outputs:
- activations: bfloat16 [768, 12288], P('narrow', 'wide')
- grad_input: float32 [768, 12288], P('narrow', 'wide')
- grad_qkv: float32 [2, 3, 768, 768], P(None, None, 'wide', 'narrow')
- grad_out: float32 [2, 768, 768], P(None, 'narrow', 'wide')
- grad_fc1: float32 [2, 768, 3072], P(None, 'wide', 'narrow')
- grad_fc2: float32 [2, 3072, 768], P(None, 'narrow', 'wide')
- grad_gains: float32 [2, 2, 768], P(None, None, ('narrow', 'wide'))
- grad_biases: float32 [2, 6, 768], P(None, None, ('narrow', 'wide'))
- grad_fc1_bias: float32 [2, 3072], P(None, ('narrow', 'wide'))
The draws below stay inside these ranges and needn't reach their ends.
Inputs may be any that keep to these rules, and one draw needn't show every extreme that they name: `clip_bounds`: row 0 is each token's clip start and row 1 its clip end (exclusive). Clips are consecutive runs of tokens that cover all 12288 tokens, each of 1 to 1500 tokens; every clip but the first and the last has 750 tokens or more, and some clip has exactly 1500.
All inputs are finite; a program needn't handle non-finite values.
Results may differ from the reference program's by a relative error of at most 0.015.
Values may be sent and summed in bfloat16 or wider, within the bound.
No kernel may reach another device: no remote copies, remote signals or barrier semaphores. Data moves between devices by JAX's collectives and lax.ppermute only.
A program may use at most 256 MiB of HBM per device.

```python
import jax
import jax.numpy as jnp
from jax import lax

D = 768
HEADS = 12
HEAD_DIM = 64
FF = 3072
CLIP = 1500
TOK_DEV = 1536
LAYERS = 2
TOKENS = 12288
N_WIDE = 8


def draw_inputs(key, part):
    key = jax.random.fold_in(key, 11)
    base_key, row_key, col_key = jax.random.split(key, 3)
    row_scale = jnp.exp(jax.random.uniform(row_key, (TOKENS, 1), jnp.float32, jnp.log(0.3), jnp.log(3.0)))
    rising = jnp.exp(jnp.log(3.0) * jnp.arange(D, dtype=jnp.float32) / D)
    col_scale = rising[None, :] * jnp.exp(jax.random.uniform(col_key, (1, D), jnp.float32, jnp.log(0.4), jnp.log(1.3)))
    values = jnp.clip(jax.random.normal(base_key, (TOKENS, D), jnp.float32), -4.0, 4.0)
    return (values * row_scale * col_scale).T.astype(jnp.bfloat16)


def draw_clip_bounds(key, part):
    key = jax.random.fold_in(key, 5)
    first_key, rest_key = jax.random.split(key)
    shortest = max(1, CLIP // 2)
    clip_slots = TOKENS // shortest + 3
    lengths = jax.random.randint(rest_key, (clip_slots,), shortest, CLIP + 1).astype(jnp.int32)
    first_len = jax.random.randint(first_key, (), 1, CLIP + 1).astype(jnp.int32)
    lengths = lengths.at[0].set(first_len)
    lengths = lengths.at[1].set(jnp.int32(CLIP))
    ends = jnp.cumsum(lengths).astype(jnp.int32)
    position = jnp.arange(TOKENS, dtype=jnp.int32)
    clip_index = jnp.searchsorted(ends, position, side='right').astype(jnp.int32)
    prior = jnp.concatenate([jnp.zeros((1,), jnp.int32), ends])
    clip_begin = prior[clip_index]
    finish = jnp.minimum(ends[clip_index], TOKENS)
    return jnp.stack([clip_begin, finish]).astype(jnp.int32)


def raised(drawn, own_key, source, target, parts, factor):
    owner, partner = [(jnp.arange(drawn.shape[dim]) // (drawn.shape[dim] // parts)).reshape([-1 if axis == dim else 1 for axis in range(drawn.ndim)]) for dim in (source, target)]
    chosen = jax.random.permutation(own_key, parts)[partner]
    strong = (owner == chosen) | (owner == (partner + parts // 2) % parts)
    return jnp.where(strong, factor * drawn, drawn)


def levels(own_key, extent, shards, smallest, largest):
    factor_of, own = 1.0, jax.random.fold_in(own_key, 6)
    for dim, parts in shards:
        draws = jnp.exp(jax.random.uniform(jax.random.fold_in(own, dim), (parts,), jnp.float32, smallest / len(shards), largest / len(shards)))
        factor_of = factor_of * jnp.repeat(draws, extent[dim] // parts).reshape([-1 if axis == dim else 1 for axis in range(len(extent))])
    return factor_of


def scatter_about(rng, shape, deviation, most, shards=(), kind=jnp.bfloat16):
    loudness = levels(rng, shape, shards, -0.22, 0.18) if shards else 1.0
    array = jax.random.normal(rng, shape, jnp.float32) * deviation * loudness
    return jnp.minimum(jnp.maximum(array, -most), most).astype(kind)


def gaussian_with(own_key, extent, scale, bound, cuts, heavy, held_as=jnp.bfloat16):
    result = scale * jax.random.normal(own_key, extent, jnp.float32)
    if cuts:
        result = result * levels(own_key, extent, cuts, -0.22, 0.18)
    return jnp.clip(raised(result, jax.random.fold_in(own_key, 3), *heavy), -bound, bound).astype(held_as)


def setup_inputs(seed: int = 0) -> dict:
    seeds = jax.random.split(jax.random.key(seed), 11)
    inputs = draw_inputs(jax.random.fold_in(seeds[10], 71), 0)
    clip_bounds = draw_clip_bounds(jax.random.fold_in(seeds[10], 71), 0)
    qkv_weight = scatter_about(seeds[2], (LAYERS, 3, D, D), D ** -0.5, 0.21875, ((2, 8), (3, 4)))
    out_weight = scatter_about(seeds[3], (LAYERS, D, D), (D // 16) ** -0.5, 0.875, ((1, 4), (2, 8)))
    fc1_weight = scatter_about(seeds[4], (LAYERS, D, FF), D ** -0.5, 0.21875, ((1, 8), (2, 4)))
    fc2_weight = scatter_about(seeds[5], (LAYERS, FF, D), FF ** -0.5, 0.109375, ((1, 4), (2, 8)))
    gains = jnp.clip(1.0 + 0.15 * jax.random.normal(seeds[6], (LAYERS, 2, D), jnp.float32), 0.25, 1.75).astype(jnp.bfloat16)
    biases = scatter_about(seeds[7], (LAYERS, 6, D), 0.3, 2.0, ((2, 32),))
    fc1_bias = scatter_about(seeds[8], (LAYERS, FF), 0.3, 2.0, ((1, 32),))
    cotangent = gaussian_with(seeds[9], (D, TOKENS), 1.0, 6.0, ((0, 4), (1, 8)), (1, 0, 8, 2.0))
    return {"inputs": inputs, "clip_bounds": clip_bounds, "qkv_weight": qkv_weight, "out_weight": out_weight, "fc1_weight": fc1_weight, "fc2_weight": fc2_weight, "gains": gains, "biases": biases, "fc1_bias": fc1_bias, "cotangent": cotangent}


EPSILON = 1e-05
MASKED = -1000000000.0
HIGHEST = lax.Precision.HIGHEST

@jax.custom_vjp
def low(v):
    return lax.optimization_barrier(v.astype(jnp.bfloat16)).astype(jnp.float32)

@jax.custom_vjp
def low_back(v):
    return v

def low_keep(v):
    return (low(v), None)

def low_pass(kept, grad):
    return (grad,)

def back_keep(v):
    return (v, None)

def back_low(kept, grad):
    return (low(grad),)
low.defvjp(low_keep, low_pass)
low_back.defvjp(back_keep, back_low)

def layer_norm(values, gain_row, shift_row):
    center = lax.optimization_barrier(jnp.mean(values, -1, keepdims=True))
    offset = values - center
    spread = lax.optimization_barrier(jnp.mean(offset * offset, -1, keepdims=True))
    return offset * lax.rsqrt(spread + EPSILON) * gain_row + shift_row

def attend(queries, key_rows, value_rows, clip_bounds):
    padding = jnp.zeros((TOK_DEV, D), jnp.float32)
    key_pad = jnp.concatenate([padding, key_rows, padding])
    value_pad = jnp.concatenate([padding, value_rows, padding])

    def attend_block(block_idx):
        first_row = block_idx * TOK_DEV
        query_block = lax.dynamic_slice_in_dim(queries, first_row, TOK_DEV, 0).reshape(TOK_DEV, HEADS, HEAD_DIM)
        key_block = lax.dynamic_slice_in_dim(key_pad, first_row, 3 * TOK_DEV, 0).reshape(3 * TOK_DEV, HEADS, HEAD_DIM)
        value_block = lax.dynamic_slice_in_dim(value_pad, first_row, 3 * TOK_DEV, 0).reshape(3 * TOK_DEV, HEADS, HEAD_DIM)
        clip_start = lax.dynamic_slice_in_dim(clip_bounds[0], first_row, TOK_DEV, 0)
        clip_end = lax.dynamic_slice_in_dim(clip_bounds[1], first_row, TOK_DEV, 0)
        key_pos = first_row - TOK_DEV + jnp.arange(3 * TOK_DEV, dtype=jnp.int32)
        inside = (key_pos[None, :] >= clip_start[:, None]) & (key_pos[None, :] < clip_end[:, None])
        scores = low_back(jnp.einsum('qhd,khd->hqk', query_block, key_block, precision=HIGHEST) * HEAD_DIM ** (-0.5))
        scores = jnp.where(inside[None], scores, MASKED)
        probabilities = low(jax.nn.softmax(scores, axis=-1))
        mixed_heads = jnp.einsum('hqk,khd->qhd', probabilities, value_block, precision=HIGHEST)
        return mixed_heads.reshape(TOK_DEV, D)
    mixed = lax.map(jax.checkpoint(attend_block), jnp.arange(N_WIDE, dtype=jnp.int32))
    return mixed.reshape(TOKENS, D)

def reference(inputs, clip_bounds, qkv_weight, out_weight, fc1_weight, fc2_weight, gains, biases, fc1_bias, cotangent):

    def forward(residual, w_qkv, w_out, w_up, w_down, gain_all, bias_all, up_bias):
        for layer_idx in range(LAYERS):
            bias_rows = bias_all[layer_idx]
            gain_pair = gain_all[layer_idx]
            normed_one = low(layer_norm(residual, gain_pair[0], bias_rows[0]))
            projected = jnp.einsum('td,kdc->ktc', normed_one, w_qkv[layer_idx], precision=HIGHEST)
            queries = low(low_back(projected[0] + bias_rows[1]))
            key_rows = low(low_back(projected[1]))
            value_rows = low(low_back(projected[2] + bias_rows[2]))
            heads_low = low(low_back(attend(queries, key_rows, value_rows, clip_bounds)))
            residual = residual + low_back(jnp.dot(heads_low, w_out[layer_idx], precision=HIGHEST)) + bias_rows[3]
            normed_two = low(layer_norm(residual, gain_pair[1], bias_rows[4]))
            hidden = low_back(jnp.dot(normed_two, w_up[layer_idx], precision=HIGHEST) + up_bias[layer_idx])
            active = low(jax.nn.gelu(hidden, approximate=False))
            residual = residual + low_back(jnp.dot(active, w_down[layer_idx], precision=HIGHEST)) + bias_rows[5]
        return residual
    output, pullback = jax.vjp(forward, inputs.astype(jnp.float32).T, qkv_weight.astype(jnp.float32), out_weight.astype(jnp.float32), fc1_weight.astype(jnp.float32), fc2_weight.astype(jnp.float32), gains.astype(jnp.float32), biases.astype(jnp.float32), fc1_bias.astype(jnp.float32))
    grads = pullback(cotangent.astype(jnp.float32).T)
    return (output.T.astype(jnp.bfloat16), grads[0].T, grads[1], grads[2], grads[3], grads[4], grads[5], grads[6], grads[7])
```

```python
import functools

import jax
import jax.numpy as jnp
from jax import lax
from jax.sharding import PartitionSpec as P

EPSILON = 1e-05
ROOT_HALF = 0.7071067811865476
INV_ROOT_TAU = 0.3989422804014327
HEAD_DIM = 64
MASKED = -1e9


def contract(left, right, left_dim, right_dim):
    return lax.dot_general(
        left, right, (((left_dim,), (right_dim,)), ((), ())), preferred_element_type=jnp.float32
    )


def window_sizes(rows):
    return [size for size in (1152, 1664, 2176, 2688, 3200) if size < rows] + [rows]


def by_window(spans, rows, branch, operands):
    sizes = window_sizes(rows)
    first = spans[0] // 128 * 128
    needed = spans[1] - first
    choice = sum((needed > size).astype(jnp.int32) for size in sizes[:-1])
    return lax.switch(
        choice,
        [
            functools.partial(
                lambda size, *given: branch(size, jnp.clip(first, 0, rows - size), *given), size
            )
            for size in sizes
        ],
        *operands,
    )


def masked_scores(query_block, key_rows, starts, ends, first):
    scores = HEAD_DIM**-0.5 * jnp.einsum(
        "qhd,khd->hqk", query_block, key_rows, preferred_element_type=jnp.float32
    )
    positions = first + jnp.arange(key_rows.shape[0], dtype=jnp.int32)
    inside = (positions[None, :] >= starts[:, None]) & (positions[None, :] < ends[:, None])
    return jnp.where(inside[None], scores, MASKED)


def attend_forward(queries, key_rows, value_rows, bounds, spans):
    def one_block(data):
        query_block, starts, ends, span = data

        def branch(size, first, query_block, starts, ends):
            keys = lax.dynamic_slice_in_dim(key_rows, first, size, 0)
            values = lax.dynamic_slice_in_dim(value_rows, first, size, 0)
            scores = masked_scores(query_block, keys, starts, ends, first)
            peak = jnp.max(scores, -1, keepdims=True)
            weights = jnp.exp(scores - peak)
            total = jnp.sum(weights, -1, keepdims=True)
            probabilities = (weights / total).astype(jnp.bfloat16)
            mixed = jnp.einsum(
                "hqk,khd->qhd", probabilities, values, preferred_element_type=jnp.float32
            )
            return mixed, (peak + jnp.log(total))[..., 0]

        return by_window(span, key_rows.shape[0], branch, (query_block, starts, ends))

    return lax.map(one_block, (queries, bounds[0], bounds[1], spans))


def attend_backward(queries, grads, inner_sums, logsums, key_rows, value_rows, bounds, spans):
    def one_block(carried, data):
        query_block, grad_block, inner, logsum, starts, ends, span = data

        def branch(size, first, key_grad, value_grad, query_block, grad_block, inner, logsum, starts, ends):
            keys = lax.dynamic_slice_in_dim(key_rows, first, size, 0)
            values = lax.dynamic_slice_in_dim(value_rows, first, size, 0)
            scores = masked_scores(query_block, keys, starts, ends, first)
            weights = jnp.exp(scores - logsum[..., None])
            weight_grad = jnp.einsum(
                "qhd,khd->hqk", grad_block, values, preferred_element_type=jnp.float32
            )
            score_grad = (weights * (weight_grad - inner[..., None])).astype(jnp.bfloat16)
            query_grad = jnp.einsum(
                "hqk,khd->qhd", score_grad, keys, preferred_element_type=jnp.float32
            )
            key_part = jnp.einsum(
                "hqk,qhd->khd", score_grad, query_block, preferred_element_type=jnp.float32
            )
            value_part = jnp.einsum(
                "hqk,qhd->khd",
                weights.astype(jnp.bfloat16),
                grad_block,
                preferred_element_type=jnp.float32,
            )
            key_part = key_part + lax.dynamic_slice_in_dim(key_grad, first, size, 0)
            value_part = value_part + lax.dynamic_slice_in_dim(value_grad, first, size, 0)
            return (
                lax.dynamic_update_slice_in_dim(key_grad, key_part, first, 0),
                lax.dynamic_update_slice_in_dim(value_grad, value_part, first, 0),
                query_grad,
            )

        key_grad, value_grad, query_grad = by_window(
            span,
            key_rows.shape[0],
            branch,
            (*carried, query_block, grad_block, inner, logsum, starts, ends),
        )
        return (key_grad, value_grad), query_grad

    zeros = jnp.zeros(key_rows.shape, jnp.float32)
    return lax.scan(
        one_block,
        (zeros, zeros),
        (queries, grads, inner_sums, logsums, bounds[0], bounds[1], spans),
    )


def walk(place):
    pair, side = divmod(place, 2)
    return 2 * pair + (side + pair) % 2


def along_path(value, step):
    count = lax.axis_size("wide")
    first, last = max(0, -step), min(count, count - step)
    return lax.ppermute(
        value, "wide", [(walk(place), walk(place + step)) for place in range(first, last)]
    )


def swap_places(value):
    count = lax.axis_size("wide")
    return lax.ppermute(value, "wide", [(walk(place), place) for place in range(count)])


def partner(value, mask):
    return lax.ppermute(value, "narrow", [(i, i ^ mask) for i in range(4)])


def gather_tokens(part):
    narrow = lax.axis_index("narrow")
    core, column = narrow % 2, narrow // 2
    across = partner(part, 2)
    both = jnp.stack([part, across])
    beside = partner(both, 1)
    mine = jnp.where(column == 0, both, both[::-1])
    other = jnp.where(column == 0, beside, beside[::-1])
    low = jnp.where(core == 0, mine, other)
    high = jnp.where(core == 0, other, mine)
    return jnp.concatenate([low[0], high[0], low[1], high[1]], axis=1)


def scatter_tokens(partial):
    narrow = lax.axis_index("narrow")
    core, column = narrow % 2, narrow // 2
    rows = partial.shape[1] // 4
    blocks = [partial[:, i * rows : (i + 1) * rows] for i in range(4)]
    even = jnp.stack([blocks[0], blocks[2]])
    odd = jnp.stack([blocks[1], blocks[3]])
    keep = jnp.where(core == 0, even, odd)
    give = jnp.where(core == 0, odd, even)
    taken = partner(give.astype(jnp.bfloat16), 1)
    pair = keep.astype(jnp.float32) + taken.astype(jnp.float32)
    keep = jnp.where(column == 0, pair[0], pair[1])
    give = jnp.where(column == 0, pair[1], pair[0])
    return keep + partner(give.astype(jnp.bfloat16), 2).astype(jnp.float32)


def swapped(value, axis, mask):
    count = lax.axis_size(axis)
    return lax.ppermute(value, axis, [(i, i ^ mask) for i in range(count)])


def gather_blocks(value, axis):
    place = 0
    mask = lax.axis_size(axis) // 2
    while mask:
        other = swapped(value, axis, mask)
        upper = (lax.axis_index(axis) & mask) != 0
        value = jnp.stack(
            [jnp.where(upper, other, value), jnp.where(upper, value, other)], axis=place
        )
        place += 1
        mask //= 2
    return value.reshape((-1,) + value.shape[place:])


def scatter_blocks(value, axis, sent):
    count = lax.axis_size(axis)
    mask = 1
    while mask < count:
        value = value.reshape((-1, 2) + value.shape[1:])
        upper = (lax.axis_index(axis) & mask) != 0
        give = jnp.where(upper, value[:, 0], value[:, 1]).astype(sent)
        keep = jnp.where(upper, value[:, 1], value[:, 0])
        value = keep.astype(jnp.float32) + swapped(give, axis, mask).astype(jnp.float32)
        mask *= 2
    return value[0]


def ordered(blocks):
    narrow = lax.axis_index("narrow")
    core, column = narrow % 2 == 1, narrow // 2 == 1
    near = [jnp.where(core, blocks[i ^ 1], blocks[i]) for i in range(4)]
    return [jnp.where(column, near[i ^ 2], near[i]) for i in range(4)]


def exchange(blocks):
    count = lax.axis_size("wide")
    received = []
    for mask, block in enumerate(ordered(blocks)):
        pairs = [(4 * w + n, 4 * walk(w) + (n ^ mask)) for w in range(count) for n in range(4)]
        received.append(lax.ppermute(block, ("wide", "narrow"), pairs))
    return ordered(received)


def features_to_tokens(value):
    rows = value.shape[1] // 4
    return jnp.concatenate(
        exchange([value[:, i * rows : (i + 1) * rows] for i in range(4)]), axis=0
    )


def tokens_to_features(value):
    rows = value.shape[0] // 4
    return jnp.concatenate(exchange([value[i * rows : (i + 1) * rows] for i in range(4)]), axis=1)


def gelu_slope(hidden):
    return (
        0.5 * (1.0 + lax.erf(hidden * ROOT_HALF))
        + hidden * jnp.exp(-0.5 * hidden * hidden) * INV_ROOT_TAU
    )


def norm_forward(values, gain, shift):
    offset = values - jnp.mean(values, 0, keepdims=True)
    inverse = lax.rsqrt(jnp.mean(offset * offset, 0, keepdims=True) + EPSILON)
    normed = offset * inverse
    return (normed * gain[:, None] + shift[:, None]).astype(jnp.bfloat16), normed, inverse


def norm_backward(upstream, normed, inverse, gain):
    scaled = upstream * gain[:, None]
    grad = inverse * (
        scaled
        - jnp.mean(scaled, 0, keepdims=True)
        - normed * jnp.mean(scaled * normed, 0, keepdims=True)
    )
    return grad, jnp.sum(upstream * normed, 1), jnp.sum(upstream, 1)


def local(
    inputs,
    clip_bounds,
    qkv_weight,
    out_weight,
    fc1_weight,
    fc2_weight,
    gains,
    biases,
    fc1_bias,
    cotangent,
):
    layers = qkv_weight.shape[0]
    width_here, tokens = inputs.shape
    d_model = 4 * width_here
    wide_count = lax.axis_size("wide")
    narrow = lax.axis_index("narrow")
    wide = lax.axis_index("wide")
    place = 2 * (wide // 2) + (wide + wide // 2) % 2
    devices = 4 * wide_count

    qkv_weights, other_weights = [], []
    for layer in range(layers):
        shard = qkv_weight[layer].transpose(1, 0, 2).reshape(-1, 3 * width_here)
        qkv_weights.append(gather_blocks(shard, "wide").reshape(d_model, -1))
        shard = jnp.concatenate(
            [fc1_weight[layer], fc2_weight[layer].T, out_weight[layer].T], axis=1
        )
        other_weights.append(gather_blocks(shard, "wide").reshape(d_model, -1))
    hidden_here = fc1_weight.shape[2]

    vectors = jnp.concatenate([gains.reshape(-1), biases.reshape(-1), fc1_bias.reshape(-1)])
    vectors = vectors.astype(jnp.float32)
    vectors = gather_blocks(vectors, "wide")
    vectors = gather_blocks(vectors, "narrow").reshape(devices, -1)
    gain_size, bias_size = gains.size, biases.size

    def whole(columns, rows):
        return columns.reshape(devices, layers, rows, -1).transpose(1, 2, 0, 3).reshape(
            layers, rows, d_model
        )

    gain_all = whole(vectors[:, :gain_size], 2)
    bias_all = whole(vectors[:, gain_size : gain_size + bias_size], 6)
    up_bias = (
        vectors[:, gain_size + bias_size :]
        .reshape(4, wide_count, layers, -1)
        .transpose(2, 0, 1, 3)
        .reshape(layers, 4, hidden_here)
    )
    up_bias = lax.dynamic_index_in_dim(up_bias, narrow, 1, False)

    q_tile = 512 if tokens % 512 == 0 else tokens
    heads_here = width_here // HEAD_DIM
    bounds = swap_places(clip_bounds) - (place - 1) * tokens
    bounds = bounds.reshape(2, -1, q_tile)
    spans = jnp.stack([bounds[0, :, 0], bounds[1, :, -1]], axis=1)

    def head_blocks(value):
        return value.reshape(-1, q_tile, heads_here, HEAD_DIM)


    residual = features_to_tokens(inputs).astype(jnp.float32)
    saved = []
    for layer in range(layers):
        bias = bias_all[layer]
        w_qkv = qkv_weights[layer]
        own_bias = lax.dynamic_slice_in_dim(bias, narrow * width_here, width_here, 1)
        low_one, normed_one, inverse_one = norm_forward(residual, gain_all[layer, 0], bias[0])
        whole_one = gather_tokens(low_one)
        kv = contract(whole_one, w_qkv[:, width_here:], 0, 0)
        kv = kv + jnp.concatenate([jnp.zeros_like(own_bias[2]), own_bias[2]])
        kv = kv.astype(jnp.bfloat16)
        kv = jnp.concatenate([along_path(kv, 1), kv, along_path(kv, -1)])
        key_rows = kv[:, :width_here].reshape(-1, heads_here, HEAD_DIM)
        value_rows = kv[:, width_here:].reshape(-1, heads_here, HEAD_DIM)
        queries = contract(whole_one, w_qkv[:, :width_here], 0, 0) + own_bias[1]
        queries = head_blocks(queries.astype(jnp.bfloat16))
        heads, logsum = attend_forward(queries, key_rows, value_rows, bounds, spans)
        low_heads = heads.reshape(tokens, width_here).astype(jnp.bfloat16)
        w_other = other_weights[layer]
        w_up, w_down, w_out = (
            w_other[:, :hidden_here],
            w_other[:, hidden_here : 2 * hidden_here],
            w_other[:, 2 * hidden_here :],
        )
        attention = scatter_tokens(contract(w_out, low_heads, 1, 1))
        middle = residual + attention + bias[3][:, None]
        low_two, normed_two, inverse_two = norm_forward(middle, gain_all[layer, 1], bias[4])
        whole_two = gather_tokens(low_two)
        hidden = contract(w_up, whole_two, 0, 0) + up_bias[layer][:, None]
        active = jax.nn.gelu(hidden, approximate=False).astype(jnp.bfloat16)
        residual = middle + scatter_tokens(contract(w_down, active, 1, 0)) + bias[5][:, None]
        saved.append(
            (
                w_qkv,
                w_out,
                w_up,
                w_down,
                whole_one,
                normed_one,
                inverse_one,
                queries,
                key_rows,
                value_rows,
                heads,
                low_heads,
                logsum,
                whole_two,
                normed_two,
                inverse_two,
                hidden,
                active,
            )
        )
    activations = tokens_to_features(residual.astype(jnp.bfloat16))

    def shared(grad):
        return scatter_blocks(
            grad.reshape(wide_count, -1, grad.shape[1]), "wide", jnp.bfloat16
        )

    gradient = features_to_tokens(cotangent).astype(jnp.float32)
    results = []
    for layer in reversed(range(layers)):
        (
            w_qkv,
            w_out,
            w_up,
            w_down,
            whole_one,
            normed_one,
            inverse_one,
            queries,
            key_rows,
            value_rows,
            heads,
            low_heads,
            logsum,
            whole_two,
            normed_two,
            inverse_two,
            hidden,
            active,
        ) = saved[layer]
        whole_grad = gather_tokens(gradient.astype(jnp.bfloat16))
        down_shift = jnp.sum(gradient, 1)
        act_grad = contract(w_down, whole_grad, 0, 0)
        hidden_grad = (act_grad * gelu_slope(hidden)).astype(jnp.bfloat16)
        two_grad = scatter_tokens(contract(w_up, hidden_grad, 1, 0))
        hidden_sum = jnp.sum(hidden_grad.astype(jnp.float32), 1)
        down_share = shared(contract(whole_grad, active, 1, 1))
        up_share = shared(contract(whole_two, hidden_grad, 1, 1))
        back_two, gain_two, shift_two = norm_backward(
            two_grad, normed_two, inverse_two, gain_all[layer, 1]
        )
        gradient = gradient + back_two
        if layer == layers - 1:
            activations, gradient = lax.optimization_barrier((activations, gradient))
        out_shift = jnp.sum(gradient, 1)
        whole_grad = gather_tokens(gradient.astype(jnp.bfloat16))
        heads_grad = head_blocks(contract(whole_grad, w_out, 0, 0).astype(jnp.bfloat16))
        out_share = shared(contract(whole_grad, low_heads, 1, 0))
        inner_sums = jnp.sum(heads_grad.astype(jnp.float32) * heads, -1).transpose(0, 2, 1)
        (key_grad, value_grad), query_grad = attend_backward(
            queries, heads_grad, inner_sums, logsum, key_rows, value_rows, bounds, spans
        )
        kv_grad = jnp.concatenate(
            [
                (key_grad * HEAD_DIM**-0.5).reshape(-1, width_here),
                value_grad.reshape(-1, width_here),
            ],
            axis=1,
        )
        from_upper = along_path(kv_grad[:tokens].astype(jnp.bfloat16), -1)
        from_lower = along_path(kv_grad[2 * tokens :].astype(jnp.bfloat16), 1)
        kv_grad = (
            kv_grad[tokens : 2 * tokens]
            + from_upper.astype(jnp.float32)
            + from_lower.astype(jnp.float32)
        )
        query_grad = (query_grad * HEAD_DIM**-0.5).reshape(tokens, width_here)
        qkv_grad = jnp.concatenate([query_grad, kv_grad], axis=1).astype(jnp.bfloat16)
        one_grad = scatter_tokens(contract(w_qkv, qkv_grad, 1, 1))
        qkv_share = shared(contract(whole_one, qkv_grad, 1, 0))
        head_sums = jnp.sum(qkv_grad.astype(jnp.float32), 0)
        back_one, gain_one, shift_one = norm_backward(
            one_grad, normed_one, inverse_one, gain_all[layer, 0]
        )
        gradient = gradient + back_one

        def placed(sums):
            return lax.dynamic_update_slice_in_dim(
                jnp.zeros((d_model,), jnp.float32), sums, narrow * width_here, 0
            )

        rows = jnp.stack(
            [
                gain_one,
                gain_two,
                shift_one,
                placed(head_sums[:width_here]),
                placed(head_sums[2 * width_here :]),
                out_shift,
                shift_two,
                down_shift,
            ]
        )
        up_sums = lax.dynamic_update_slice_in_dim(
            jnp.zeros((4, hidden_here), jnp.float32), hidden_sum[None], narrow, 0
        )
        small = jnp.concatenate(
            [
                rows.reshape(8, devices, -1).transpose(1, 0, 2).reshape(devices, -1),
                up_sums.reshape(devices, -1),
            ],
            axis=1,
        )
        results.append((qkv_share, out_share, up_share, down_share, small))
    results = results[::-1]
    grad_input = tokens_to_features(gradient.astype(jnp.bfloat16)).astype(jnp.float32)
    small = jnp.stack([entry[4] for entry in results], axis=1)
    small = scatter_blocks(
        small.reshape((4, wide_count) + small.shape[1:]), "narrow", jnp.float32
    )
    small = scatter_blocks(small, "wide", jnp.float32)
    row_part = small[:, : 8 * gains.shape[2]].reshape(layers, 8, -1)
    qkv, out, up, down = (jnp.stack([entry[i] for entry in results]) for i in range(4))
    return (
        activations,
        grad_input,
        qkv.reshape(layers, -1, 3, width_here).transpose(0, 2, 1, 3),
        out.transpose(0, 2, 1),
        up,
        down.transpose(0, 2, 1),
        row_part[:, :2],
        row_part[:, 2:],
        small[:, 8 * gains.shape[2] :],
    )


def solution(mesh):
    in_specs = (
        P("narrow", "wide"),
        P(None, "wide"),
        P(None, None, "wide", "narrow"),
        P(None, "narrow", "wide"),
        P(None, "wide", "narrow"),
        P(None, "narrow", "wide"),
        P(None, None, ("narrow", "wide")),
        P(None, None, ("narrow", "wide")),
        P(None, ("narrow", "wide")),
        P("narrow", "wide"),
    )
    out_specs = (
        P("narrow", "wide"),
        P("narrow", "wide"),
        P(None, None, "wide", "narrow"),
        P(None, "narrow", "wide"),
        P(None, "wide", "narrow"),
        P(None, "narrow", "wide"),
        P(None, None, ("narrow", "wide")),
        P(None, None, ("narrow", "wide")),
        P(None, ("narrow", "wide")),
    )
    return jax.shard_map(local, mesh=mesh, in_specs=in_specs, out_specs=out_specs, check_vma=False)
```

```python
import jax
import jax.numpy as jnp
from jax import lax
from jax.sharding import PartitionSpec as P

EPSILON = 1e-05
ROOT_HALF = 0.7071067811865476
INV_ROOT_TAU = 0.3989422804014327
HEAD_DIM = 64
MASKED = -1e9


def contract(left, right, left_dim, right_dim):
    return lax.dot_general(
        left, right, (((left_dim,), (right_dim,)), ((), ())), preferred_element_type=jnp.float32
    )


def windows(queries, key_rows):
    blocks, rows = queries.shape[:2]
    size = rows + 2 * (key_rows.shape[0] // 3)
    return [slice(i * rows, i * rows + size) for i in range(blocks)]


def masked_scores(query_block, key_rows, starts, ends, first):
    scores = HEAD_DIM**-0.5 * jnp.einsum(
        "qhd,khd->hqk", query_block, key_rows, preferred_element_type=jnp.float32
    )
    positions = first + jnp.arange(key_rows.shape[0], dtype=jnp.int32)
    inside = (positions[None, :] >= starts[:, None]) & (positions[None, :] < ends[:, None])
    return jnp.where(inside[None], scores, MASKED)


def attend_forward(queries, key_rows, value_rows, bounds):
    mixed, logsums = [], []
    for i, window in enumerate(windows(queries, key_rows)):
        scores = masked_scores(
            queries[i], key_rows[window], bounds[0, i], bounds[1, i], window.start
        )
        peak = jnp.max(scores, -1, keepdims=True)
        weights = jnp.exp(scores - peak)
        total = jnp.sum(weights, -1, keepdims=True)
        probabilities = (weights / total).astype(jnp.bfloat16)
        mixed.append(
            jnp.einsum(
                "hqk,khd->qhd",
                probabilities,
                value_rows[window],
                preferred_element_type=jnp.float32,
            )
        )
        logsums.append((peak + jnp.log(total))[..., 0])
    return jnp.stack(mixed), logsums


def attend_backward(queries, grads, inner_sums, logsums, key_rows, value_rows, bounds):
    query_grads, key_grad, value_grad = [], 0.0, 0.0
    for i, window in enumerate(windows(queries, key_rows)):
        keys, values = key_rows[window], value_rows[window]
        scores = masked_scores(queries[i], keys, bounds[0, i], bounds[1, i], window.start)
        weights = jnp.exp(scores - logsums[i][..., None])
        weight_grad = jnp.einsum(
            "qhd,khd->hqk", grads[i], values, preferred_element_type=jnp.float32
        )
        score_grad = (weights * (weight_grad - inner_sums[i][..., None])).astype(jnp.bfloat16)
        query_grads.append(
            jnp.einsum("hqk,khd->qhd", score_grad, keys, preferred_element_type=jnp.float32)
        )
        key_part = jnp.einsum(
            "hqk,qhd->khd", score_grad, queries[i], preferred_element_type=jnp.float32
        )
        value_part = jnp.einsum(
            "hqk,qhd->khd",
            weights.astype(jnp.bfloat16),
            grads[i],
            preferred_element_type=jnp.float32,
        )
        around = ((window.start, key_rows.shape[0] - window.stop), (0, 0), (0, 0))
        key_grad = key_grad + jnp.pad(key_part, around)
        value_grad = value_grad + jnp.pad(value_part, around)
    return (key_grad, value_grad), jnp.stack(query_grads)


def walk(place):
    pair, side = divmod(place, 2)
    return 2 * pair + (side + pair) % 2


def along_path(value, step):
    count = lax.axis_size("wide")
    first, last = max(0, -step), min(count, count - step)
    return lax.ppermute(
        value, "wide", [(walk(place), walk(place + step)) for place in range(first, last)]
    )


def swap_places(value):
    count = lax.axis_size("wide")
    return lax.ppermute(value, "wide", [(walk(place), place) for place in range(count)])


def partner(value, mask):
    return lax.ppermute(value, "narrow", [(i, i ^ mask) for i in range(4)])


def gather_tokens(part):
    narrow = lax.axis_index("narrow")
    core, column = narrow % 2, narrow // 2
    across = partner(part, 2)
    both = jnp.stack([part, across])
    beside = partner(both, 1)
    mine = jnp.where(column == 0, both, both[::-1])
    other = jnp.where(column == 0, beside, beside[::-1])
    low = jnp.where(core == 0, mine, other)
    high = jnp.where(core == 0, other, mine)
    return jnp.concatenate([low[0], high[0], low[1], high[1]], axis=1)


def scatter_tokens(partial):
    narrow = lax.axis_index("narrow")
    core, column = narrow % 2, narrow // 2
    rows = partial.shape[1] // 4
    blocks = [partial[:, i * rows : (i + 1) * rows] for i in range(4)]
    even = jnp.stack([blocks[0], blocks[2]])
    odd = jnp.stack([blocks[1], blocks[3]])
    keep = jnp.where(core == 0, even, odd)
    give = jnp.where(core == 0, odd, even)
    taken = partner(give.astype(jnp.bfloat16), 1)
    pair = keep.astype(jnp.float32) + taken.astype(jnp.float32)
    keep = jnp.where(column == 0, pair[0], pair[1])
    give = jnp.where(column == 0, pair[1], pair[0])
    return keep + partner(give.astype(jnp.bfloat16), 2).astype(jnp.float32)


def swapped(value, axis, mask):
    count = lax.axis_size(axis)
    return lax.ppermute(value, axis, [(i, i ^ mask) for i in range(count)])


def gather_blocks(value, axis):
    place = 0
    mask = lax.axis_size(axis) // 2
    while mask:
        other = swapped(value, axis, mask)
        upper = (lax.axis_index(axis) & mask) != 0
        value = jnp.stack(
            [jnp.where(upper, other, value), jnp.where(upper, value, other)], axis=place
        )
        place += 1
        mask //= 2
    return value.reshape((-1,) + value.shape[place:])


def scatter_blocks(value, axis, sent):
    count = lax.axis_size(axis)
    mask = 1
    while mask < count:
        value = value.reshape((-1, 2) + value.shape[1:])
        upper = (lax.axis_index(axis) & mask) != 0
        give = jnp.where(upper, value[:, 0], value[:, 1]).astype(sent)
        keep = jnp.where(upper, value[:, 1], value[:, 0])
        value = keep.astype(jnp.float32) + swapped(give, axis, mask).astype(jnp.float32)
        mask *= 2
    return value[0]


def ordered(blocks):
    narrow = lax.axis_index("narrow")
    core, column = narrow % 2 == 1, narrow // 2 == 1
    near = [jnp.where(core, blocks[i ^ 1], blocks[i]) for i in range(4)]
    return [jnp.where(column, near[i ^ 2], near[i]) for i in range(4)]


def exchange(blocks):
    count = lax.axis_size("wide")
    received = []
    for mask, block in enumerate(ordered(blocks)):
        pairs = [(4 * w + n, 4 * walk(w) + (n ^ mask)) for w in range(count) for n in range(4)]
        received.append(lax.ppermute(block, ("wide", "narrow"), pairs))
    return ordered(received)


def features_to_tokens(value):
    rows = value.shape[1] // 4
    return jnp.concatenate(
        exchange([value[:, i * rows : (i + 1) * rows] for i in range(4)]), axis=0
    )


def tokens_to_features(value):
    rows = value.shape[0] // 4
    return jnp.concatenate(exchange([value[i * rows : (i + 1) * rows] for i in range(4)]), axis=1)


def gelu_slope(hidden):
    return (
        0.5 * (1.0 + lax.erf(hidden * ROOT_HALF))
        + hidden * jnp.exp(-0.5 * hidden * hidden) * INV_ROOT_TAU
    )


def norm_forward(values, gain, shift):
    offset = values - jnp.mean(values, 0, keepdims=True)
    inverse = lax.rsqrt(jnp.mean(offset * offset, 0, keepdims=True) + EPSILON)
    normed = offset * inverse
    return (normed * gain[:, None] + shift[:, None]).astype(jnp.bfloat16), normed, inverse


def norm_backward(upstream, normed, inverse, gain):
    scaled = upstream * gain[:, None]
    grad = inverse * (
        scaled
        - jnp.mean(scaled, 0, keepdims=True)
        - normed * jnp.mean(scaled * normed, 0, keepdims=True)
    )
    return grad, jnp.sum(upstream * normed, 1), jnp.sum(upstream, 1)


def local(
    inputs,
    clip_bounds,
    qkv_weight,
    out_weight,
    fc1_weight,
    fc2_weight,
    gains,
    biases,
    fc1_bias,
    cotangent,
):
    layers = qkv_weight.shape[0]
    width_here, tokens = inputs.shape
    d_model = 4 * width_here
    wide_count = lax.axis_size("wide")
    narrow = lax.axis_index("narrow")
    wide = lax.axis_index("wide")
    place = 2 * (wide // 2) + (wide + wide // 2) % 2
    devices = 4 * wide_count

    qkv_weights, other_weights = [], []
    for layer in range(layers):
        shard = qkv_weight[layer].transpose(1, 0, 2).reshape(-1, 3 * width_here)
        qkv_weights.append(gather_blocks(shard, "wide").reshape(d_model, -1))
        shard = jnp.concatenate(
            [fc1_weight[layer], fc2_weight[layer].T, out_weight[layer].T], axis=1
        )
        other_weights.append(gather_blocks(shard, "wide").reshape(d_model, -1))
    hidden_here = fc1_weight.shape[2]

    vectors = jnp.concatenate([gains.reshape(-1), biases.reshape(-1), fc1_bias.reshape(-1)])
    vectors = vectors.astype(jnp.float32)
    vectors = gather_blocks(vectors, "wide")
    vectors = gather_blocks(vectors, "narrow").reshape(devices, -1)
    gain_size, bias_size = gains.size, biases.size

    def whole(columns, rows):
        return columns.reshape(devices, layers, rows, -1).transpose(1, 2, 0, 3).reshape(
            layers, rows, d_model
        )

    gain_all = whole(vectors[:, :gain_size], 2)
    bias_all = whole(vectors[:, gain_size : gain_size + bias_size], 6)
    up_bias = (
        vectors[:, gain_size + bias_size :]
        .reshape(4, wide_count, layers, -1)
        .transpose(2, 0, 1, 3)
        .reshape(layers, 4, hidden_here)
    )
    up_bias = lax.dynamic_index_in_dim(up_bias, narrow, 1, False)

    q_tile = 512 if tokens % 512 == 0 else tokens
    heads_here = width_here // HEAD_DIM
    bounds = swap_places(clip_bounds) - (place - 1) * tokens
    bounds = bounds.reshape(2, -1, q_tile)

    def head_blocks(value):
        return value.reshape(-1, q_tile, heads_here, HEAD_DIM)


    residual = features_to_tokens(inputs).astype(jnp.float32)
    saved = []
    for layer in range(layers):
        bias = bias_all[layer]
        w_qkv = qkv_weights[layer]
        own_bias = lax.dynamic_slice_in_dim(bias, narrow * width_here, width_here, 1)
        low_one, normed_one, inverse_one = norm_forward(residual, gain_all[layer, 0], bias[0])
        whole_one = gather_tokens(low_one)
        kv = contract(whole_one, w_qkv[:, width_here:], 0, 0)
        kv = kv + jnp.concatenate([jnp.zeros_like(own_bias[2]), own_bias[2]])
        kv = kv.astype(jnp.bfloat16)
        kv = jnp.concatenate([along_path(kv, 1), kv, along_path(kv, -1)])
        key_rows = kv[:, :width_here].reshape(-1, heads_here, HEAD_DIM)
        value_rows = kv[:, width_here:].reshape(-1, heads_here, HEAD_DIM)
        queries = contract(whole_one, w_qkv[:, :width_here], 0, 0) + own_bias[1]
        queries = head_blocks(queries.astype(jnp.bfloat16))
        heads, logsum = attend_forward(queries, key_rows, value_rows, bounds)
        low_heads = heads.reshape(tokens, width_here).astype(jnp.bfloat16)
        w_other = other_weights[layer]
        w_up, w_down, w_out = (
            w_other[:, :hidden_here],
            w_other[:, hidden_here : 2 * hidden_here],
            w_other[:, 2 * hidden_here :],
        )
        attention = scatter_tokens(contract(w_out, low_heads, 1, 1))
        middle = residual + attention + bias[3][:, None]
        low_two, normed_two, inverse_two = norm_forward(middle, gain_all[layer, 1], bias[4])
        whole_two = gather_tokens(low_two)
        hidden = contract(w_up, whole_two, 0, 0) + up_bias[layer][:, None]
        active = jax.nn.gelu(hidden, approximate=False).astype(jnp.bfloat16)
        residual = middle + scatter_tokens(contract(w_down, active, 1, 0)) + bias[5][:, None]
        saved.append(
            (
                w_qkv,
                w_out,
                w_up,
                w_down,
                whole_one,
                normed_one,
                inverse_one,
                queries,
                key_rows,
                value_rows,
                heads,
                low_heads,
                logsum,
                whole_two,
                normed_two,
                inverse_two,
                hidden,
                active,
            )
        )
    activations = tokens_to_features(residual.astype(jnp.bfloat16))

    def shared(grad):
        return scatter_blocks(
            grad.reshape(wide_count, -1, grad.shape[1]), "wide", jnp.bfloat16
        )

    gradient = features_to_tokens(cotangent).astype(jnp.float32)
    results = []
    for layer in reversed(range(layers)):
        (
            w_qkv,
            w_out,
            w_up,
            w_down,
            whole_one,
            normed_one,
            inverse_one,
            queries,
            key_rows,
            value_rows,
            heads,
            low_heads,
            logsum,
            whole_two,
            normed_two,
            inverse_two,
            hidden,
            active,
        ) = saved[layer]
        whole_grad = gather_tokens(gradient.astype(jnp.bfloat16))
        down_shift = jnp.sum(gradient, 1)
        act_grad = contract(w_down, whole_grad, 0, 0)
        hidden_grad = (act_grad * gelu_slope(hidden)).astype(jnp.bfloat16)
        two_grad = scatter_tokens(contract(w_up, hidden_grad, 1, 0))
        hidden_sum = jnp.sum(hidden_grad.astype(jnp.float32), 1)
        down_share = shared(contract(whole_grad, active, 1, 1))
        up_share = shared(contract(whole_two, hidden_grad, 1, 1))
        back_two, gain_two, shift_two = norm_backward(
            two_grad, normed_two, inverse_two, gain_all[layer, 1]
        )
        gradient = gradient + back_two
        if layer == layers - 1:
            activations, gradient = lax.optimization_barrier((activations, gradient))
        out_shift = jnp.sum(gradient, 1)
        whole_grad = gather_tokens(gradient.astype(jnp.bfloat16))
        heads_grad = head_blocks(contract(whole_grad, w_out, 0, 0).astype(jnp.bfloat16))
        out_share = shared(contract(whole_grad, low_heads, 1, 0))
        inner_sums = jnp.sum(heads_grad.astype(jnp.float32) * heads, -1).transpose(0, 2, 1)
        (key_grad, value_grad), query_grad = attend_backward(
            queries, heads_grad, inner_sums, logsum, key_rows, value_rows, bounds
        )
        kv_grad = jnp.concatenate(
            [
                (key_grad * HEAD_DIM**-0.5).reshape(-1, width_here),
                value_grad.reshape(-1, width_here),
            ],
            axis=1,
        )
        from_upper = along_path(kv_grad[:tokens].astype(jnp.bfloat16), -1)
        from_lower = along_path(kv_grad[2 * tokens :].astype(jnp.bfloat16), 1)
        kv_grad = (
            kv_grad[tokens : 2 * tokens]
            + from_upper.astype(jnp.float32)
            + from_lower.astype(jnp.float32)
        )
        query_grad = (query_grad * HEAD_DIM**-0.5).reshape(tokens, width_here)
        qkv_grad = jnp.concatenate([query_grad, kv_grad], axis=1).astype(jnp.bfloat16)
        one_grad = scatter_tokens(contract(w_qkv, qkv_grad, 1, 1))
        qkv_share = shared(contract(whole_one, qkv_grad, 1, 0))
        head_sums = jnp.sum(qkv_grad.astype(jnp.float32), 0)
        back_one, gain_one, shift_one = norm_backward(
            one_grad, normed_one, inverse_one, gain_all[layer, 0]
        )
        gradient = gradient + back_one

        def placed(sums):
            return lax.dynamic_update_slice_in_dim(
                jnp.zeros((d_model,), jnp.float32), sums, narrow * width_here, 0
            )

        rows = jnp.stack(
            [
                gain_one,
                gain_two,
                shift_one,
                placed(head_sums[:width_here]),
                placed(head_sums[2 * width_here :]),
                out_shift,
                shift_two,
                down_shift,
            ]
        )
        up_sums = lax.dynamic_update_slice_in_dim(
            jnp.zeros((4, hidden_here), jnp.float32), hidden_sum[None], narrow, 0
        )
        small = jnp.concatenate(
            [
                rows.reshape(8, devices, -1).transpose(1, 0, 2).reshape(devices, -1),
                up_sums.reshape(devices, -1),
            ],
            axis=1,
        )
        results.append((qkv_share, out_share, up_share, down_share, small))
    results = results[::-1]
    grad_input = tokens_to_features(gradient.astype(jnp.bfloat16)).astype(jnp.float32)
    small = jnp.stack([entry[4] for entry in results], axis=1)
    small = scatter_blocks(
        small.reshape((4, wide_count) + small.shape[1:]), "narrow", jnp.float32
    )
    small = scatter_blocks(small, "wide", jnp.float32)
    row_part = small[:, : 8 * gains.shape[2]].reshape(layers, 8, -1)
    qkv, out, up, down = (jnp.stack([entry[i] for entry in results]) for i in range(4))
    return (
        activations,
        grad_input,
        qkv.reshape(layers, -1, 3, width_here).transpose(0, 2, 1, 3),
        out.transpose(0, 2, 1),
        up,
        down.transpose(0, 2, 1),
        row_part[:, :2],
        row_part[:, 2:],
        small[:, 8 * gains.shape[2] :],
    )


def solution(mesh):
    in_specs = (
        P("narrow", "wide"),
        P(None, "wide"),
        P(None, None, "wide", "narrow"),
        P(None, "narrow", "wide"),
        P(None, "wide", "narrow"),
        P(None, "narrow", "wide"),
        P(None, None, ("narrow", "wide")),
        P(None, None, ("narrow", "wide")),
        P(None, ("narrow", "wide")),
        P("narrow", "wide"),
    )
    out_specs = (
        P("narrow", "wide"),
        P("narrow", "wide"),
        P(None, None, "wide", "narrow"),
        P(None, "narrow", "wide"),
        P(None, "wide", "narrow"),
        P(None, "narrow", "wide"),
        P(None, None, ("narrow", "wide")),
        P(None, None, ("narrow", "wide")),
        P(None, ("narrow", "wide")),
    )
    return jax.shard_map(local, mesh=mesh, in_specs=in_specs, out_specs=out_specs, check_vma=False)
```
